256 devices in a mesh: seq: 32 (over y_hi, z, core), chan: 8 (over y_lo, x).
Axes of the slice: x: 4, y: 4 (y_hi: 2, y_lo: 2; y = y_hi * 2 + y_lo), z: 8, core: 2. Of those that a mesh axis runs over, the one named last changes fastest.
Arguments:
- tokens: bfloat16 [131072, 1024], P('seq', 'chan'), may hold values from -9 to 9
- gain_in: float32 [1024], P('chan'), may hold values from 0.1 to 1.9
- right_in: bfloat16 [512, 512], replicated, may hold values from -0.25 to 0.25
- twiddle_in: float32 [256, 512], P('seq'), may hold values from -1.5 to 1.5
- left_in: bfloat16 [256, 256], replicated, may hold values from -0.375 to 0.375
- kernel: bfloat16 [256, 512, 1024], P(None, 'seq', 'chan'), may hold values from -5 to 5
- left_out: bfloat16 [256, 256], replicated, may hold values from -0.375 to 0.375
- right_out: bfloat16 [512, 512], replicated, may hold values from -0.25 to 0.25
- twiddle_out: float32 [256, 512], P('seq'), may hold values from -1.5 to 1.5
- gain_mlp: float32 [1024], replicated, may hold values from 0.1 to 1.9
- w_gate: bfloat16 [1024, 4096], P(None, 'chan'), may hold values from -0.1875 to 0.1875
- w_up: bfloat16 [1024, 4096], P(None, 'chan'), may hold values from -0.1875 to 0.1875
- w_down: bfloat16 [4096, 1024], P('chan'), may hold values from -0.09375 to 0.09375
Outputs:
- layer_out: bfloat16 [131072, 1024], P('seq', 'chan')
The draws below stay inside these ranges and needn't reach their ends.
All inputs are finite; a program needn't handle non-finite values.
Results may differ from the reference program's by a relative error of at most 0.013.
Values may be sent and summed in bfloat16 or wider, within the bound.
No kernel may reach another device: no remote copies, remote signals or barrier semaphores. Data moves between devices by JAX's collectives and lax.ppermute only.
A program may use at most 128 MiB of HBM per device.

```python
import math
import jax
import jax.numpy as jnp
from jax import lax

P_SIZE = 256
Q = 512
D = 1024
HID = 4096
N_CHAN = 8


def draw_tokens(key, part):
    key = jax.random.fold_in(key, 11)
    column = jnp.arange(D, dtype=jnp.float32) / max(D - 1, 1)
    col_scale = 0.5 * jnp.exp(jnp.log(3.0) * column)
    base = jnp.clip(jax.random.normal(key, (P_SIZE * Q, D), jnp.float32), -4.0, 4.0)
    values = base * col_scale[None, :]
    return values.astype(jnp.bfloat16)


def steps_of(stream_key, extent, split, least, high):
    gain, own = 1.0, jax.random.fold_in(stream_key, 6)
    for dim, blocks in split:
        draws = jnp.exp(jax.random.uniform(jax.random.fold_in(own, dim), (blocks,), jnp.float32, least / len(split), high / len(split)))
        gain = gain * jnp.repeat(draws, extent[dim] // blocks).reshape([-1 if axis == dim else 1 for axis in range(len(extent))])
    return gain


def bell_draw(stream_key, shape, width, limit, shards=(), kind=jnp.bfloat16):
    entries = jax.random.normal(stream_key, shape, jnp.float32) * width
    if len(shards) > 0:
        entries = steps_of(stream_key, shape, shards, -0.22, 0.18) * entries
    return jnp.clip(entries, min=-limit, max=limit).astype(kind)


def setup_inputs(seed: int = 0) -> dict:
    key_of = jax.random.split(jax.random.key(seed), 14)
    return {
        "tokens": draw_tokens(jax.random.fold_in(key_of[13], 71), 0),
        "gain_in": jnp.clip(1.0 + 0.18 * jax.random.normal(key_of[1], (D,), jnp.float32), 0.1, 1.9),
        "right_in": bell_draw(key_of[2], (Q, Q), Q ** -0.5, 0.25),
        "twiddle_in": jnp.clip(jax.random.uniform(key_of[3], (P_SIZE, Q), jnp.float32, -1.5, 1.5) * steps_of(key_of[3], (P_SIZE, Q), ((0, 32),), -0.4, 0.0), -1.5, 1.5),
        "left_in": bell_draw(key_of[4], (P_SIZE, P_SIZE), P_SIZE ** -0.5, 0.375),
        "kernel": bell_draw(key_of[5], (P_SIZE, Q, D), 1.0, 5.0, ((1, 32), (2, 8))),
        "left_out": bell_draw(key_of[6], (P_SIZE, P_SIZE), P_SIZE ** -0.5, 0.375),
        "right_out": bell_draw(key_of[7], (Q, Q), Q ** -0.5, 0.25),
        "twiddle_out": jnp.clip(jax.random.uniform(key_of[8], (P_SIZE, Q), jnp.float32, -1.5, 1.5) * steps_of(key_of[8], (P_SIZE, Q), ((0, 32),), -0.4, 0.0), -1.5, 1.5),
        "gain_mlp": jnp.clip(1.0 + 0.18 * jax.random.normal(key_of[9], (D,), jnp.float32), 0.1, 1.9),
        "w_gate": bell_draw(key_of[10], (D, HID), D ** -0.5, 0.1875, ((1, 8),)),
        "w_up": bell_draw(key_of[11], (D, HID), D ** -0.5, 0.1875, ((1, 8),)),
        "w_down": bell_draw(key_of[12], (HID, D), HID ** -0.5, 0.09375, ((0, 8),)),
    }


epsilon = 1e-06

def reference(tokens, gain_in, right_in, twiddle_in, left_in, kernel, left_out, right_out, twiddle_out, gain_mlp, w_gate, w_up, w_down):
    tok_float = tokens.astype(jnp.float32)
    row_scale = lax.rsqrt(lax.optimization_barrier(jnp.mean(tok_float * tok_float, axis=1, keepdims=True)) + epsilon)
    normed_in = (tok_float * row_scale * gain_in.astype(jnp.float32)).astype(jnp.bfloat16).reshape(P_SIZE, Q, D)
    factor_one = jnp.einsum('rq,pqd->prd', right_in.astype(jnp.float32), normed_in.astype(jnp.float32))
    factor_one = (factor_one * twiddle_in[:, :, None]).astype(jnp.bfloat16)
    factor_two = jnp.einsum('sp,prd->srd', left_in.astype(jnp.float32), factor_one.astype(jnp.float32))
    factor_two = (factor_two * kernel.astype(jnp.float32)).astype(jnp.bfloat16)
    factor_three = jnp.einsum('ts,srd->trd', left_out.astype(jnp.float32), factor_two.astype(jnp.float32)).astype(jnp.bfloat16)
    mixed = jnp.einsum('ur,prd->pud', right_out.astype(jnp.float32), factor_three.astype(jnp.float32))
    mixed = mixed * twiddle_out[:, :, None]
    stream = (tok_float + mixed.reshape(P_SIZE * Q, D)).astype(jnp.bfloat16)
    block_len = math.gcd(P_SIZE * Q, 4096)
    group_len = HID // N_CHAN
    down_groups = w_down.reshape(N_CHAN, group_len, D)

    def block_mlp(block_rows):
        rows_float = block_rows.astype(jnp.float32)
        scale_mlp = lax.rsqrt(lax.optimization_barrier(jnp.mean(rows_float * rows_float, axis=1, keepdims=True)) + epsilon)
        normed_mlp = (rows_float * scale_mlp * gain_mlp.astype(jnp.float32)).astype(jnp.bfloat16)
        gate_proj = jnp.dot(normed_mlp, w_gate, preferred_element_type=jnp.float32)
        up_proj = jnp.dot(normed_mlp, w_up, preferred_element_type=jnp.float32)
        hidden = (jax.nn.silu(gate_proj) * up_proj).astype(jnp.bfloat16)
        running = jnp.zeros((block_len, D), jnp.float32)
        for group in range(N_CHAN):
            contrib = jnp.dot(hidden[:, group * group_len:(group + 1) * group_len], down_groups[group], preferred_element_type=jnp.float32)
            contrib = lax.optimization_barrier(contrib.astype(jnp.bfloat16))
            running = running + contrib.astype(jnp.float32)
        return (rows_float + running).astype(jnp.bfloat16)
    blocks = stream.reshape(P_SIZE * Q // block_len, block_len, D)
    return lax.map(block_mlp, blocks).reshape(P_SIZE * Q, D)
```

```python
import functools

import jax
import jax.numpy as jnp
from jax import lax
from jax.experimental import pallas as pl
from jax.experimental.pallas import tpu as pltpu
from jax.sharding import PartitionSpec as P

EPS = 1e-06
BOTH = ("seq", "chan")
Z, CORE, YLO, X = 8, 2, 2, 4
YHI = 2
BF, F32 = jnp.bfloat16, jnp.float32


def route(move):
    pairs = []
    for yhi in range(YHI):
        for z in range(Z):
            for core in range(CORE):
                for ylo in range(YLO):
                    for x in range(X):
                        a, b, c, d, e = move(yhi, z, core, ylo, x)
                        src = (((yhi * Z + z) * CORE + core) * YLO + ylo) * X + x
                        dst = (((a * Z + b) * CORE + c) * YLO + d) * X + e
                        pairs.append((src, dst))
    return pairs


def along_x(sign):
    def move(yhi, z, core, ylo, x):
        step = sign if core == 0 else -sign
        return yhi, z, core, ylo, (x + step) % X

    return route(move)


def along_y(yhi, z, core, ylo, x):
    y = (yhi * YLO + ylo + (1 if core == 0 else -1)) % (YHI * YLO)
    return y // YLO, z, core, y % YLO, x


def other_core(yhi, z, core, ylo, x):
    return yhi, z, 1 - core, ylo, x


def first_kernel(place, tok, right, tw, out):
    groups, rows, width = tok.shape
    energy = jnp.zeros((rows, 1), F32)
    for g in range(groups):
        t = tok[g].astype(F32)
        energy = energy + jnp.sum(t * t, axis=1, keepdims=True)
    scale = lax.rsqrt(energy / (groups * width) + EPS)
    turned = tw[...].T
    lane = lax.broadcasted_iota(jnp.int32, turned.shape, 1)
    twiddle = jnp.sum(jnp.where(lane == place[0], turned, 0.0), axis=1, keepdims=True)
    for g in range(0, groups, 2):
        pair = [(tok[g + k].astype(F32) * scale).astype(BF) for k in range(2)]
        f = jnp.dot(right[...], jnp.concatenate(pair, axis=1), preferred_element_type=F32)
        f = (f * twiddle).astype(BF)
        for k in range(2):
            part = f[:, k * width : (k + 1) * width]
            out[:, g + k] = part.reshape(out.shape[0], out.shape[2], width)


def middle_kernel(col, left_in, left_out, kern, gain, out, flat, kflat):
    blocks, inner, width = col.shape
    flat[...] = col[...].astype(F32).reshape(blocks * inner, width)
    kflat[...] = (kern[...].astype(F32) * gain[...][None]).reshape(blocks * inner, width)
    for r in range(0, inner, 2):
        at = [pl.ds(r + k, blocks, stride=inner) for k in range(2)]
        x = jnp.concatenate([flat[a, :].astype(BF) for a in at], axis=1)
        k = jnp.concatenate([kflat[a, :] for a in at], axis=1)
        two = jnp.dot(left_in[...], x, preferred_element_type=F32)
        two = (two * k).astype(BF)
        three = jnp.dot(left_out[...], two, preferred_element_type=F32)
        for i, a in enumerate(at):
            flat[a, :] = three[:, i * width : (i + 1) * width]
    out[...] = flat[...].reshape(blocks, inner, width).astype(BF)


def last_kernel(count, place, back, tok, right, tw, gain, *rest):
    packs, out = rest[:count], rest[count]
    weights, acc, normed, sems = rest[count + 1 :]
    for i in range(count):
        pltpu.make_async_copy(packs[i], weights.at[i], sems.at[i]).start()
    groups, rows, width = tok.shape
    full = groups * width
    turned = tw[...].T
    lane = lax.broadcasted_iota(jnp.int32, turned.shape, 1)
    twiddle = jnp.sum(jnp.where(lane == place[0], turned, 0.0), axis=1, keepdims=True)
    energy = jnp.zeros((rows, 1), F32)
    for g in range(0, groups, 2):
        pair = [back[:, g + k].reshape(rows, width) for k in range(2)]
        mixed = jnp.dot(right[...], jnp.concatenate(pair, axis=1), preferred_element_type=F32)
        mixed = mixed * twiddle
        for k in range(2):
            at = pl.ds((g + k) * width, width)
            s = (tok[g + k].astype(F32) + mixed[:, k * width : (k + 1) * width]).astype(BF).astype(F32)
            acc[:, at] = s
            energy = energy + jnp.sum(s * s, axis=1, keepdims=True)
    scale = lax.rsqrt(energy / full + EPS)
    normed[...] = (acc[...] * scale * gain[...]).astype(BF)
    hid = weights.shape[2] // 2

    @pl.loop(0, count)
    def _(i):
        pltpu.make_async_copy(packs[0], weights.at[i], sems.at[i]).wait()
        both = jnp.dot(normed[...], weights[i, :full, :], preferred_element_type=F32)
        gate, up = both[:, :hid], both[:, hid:]
        hidden = (gate * up / (1.0 + jnp.exp(-gate))).astype(BF)
        half = full // 2
        for k in range(2):
            down = weights[i, full + k * hid : full + (k + 1) * hid, :]
            acc[:, k * half : (k + 1) * half] += jnp.dot(hidden, down, preferred_element_type=F32)

    for g in range(groups):
        out[g] = acc[:, g * width : (g + 1) * width].astype(BF)


def local(tokens, gain_in, right_in, twiddle_in, left_in, kernel, left_out, right_out, twiddle_out, gain_mlp, w_gate, w_up, w_down):
    own = tokens.shape[1]
    inner = right_in.shape[0]
    n_chan = lax.axis_size("chan")
    n_seq = lax.axis_size("seq")
    blocks = left_in.shape[0]
    full = own * n_chan
    r_own = kernel.shape[1]
    hid = w_gate.shape[1] // 2
    place = lax.axis_index("chan").astype(jnp.int32)[None]
    core = lax.axis_index("seq") % CORE

    vmem = pl.BlockSpec(memory_space=pltpu.VMEM)
    smem = pl.BlockSpec(memory_space=pltpu.SMEM)
    any_ = pl.BlockSpec(memory_space=pl.ANY)

    tok = lax.all_to_all(tokens.reshape(n_chan, inner, own), "chan", 0, 0, tiled=True)

    def pack(side):
        at = side * hid
        cut = lambda w, axis: lax.dynamic_slice_in_dim(w, at, hid, axis)
        d = cut(w_down, 0)
        up = jnp.concatenate([cut(w_gate, 1), cut(w_up, 1)], axis=1)
        return jnp.concatenate([up, d[:, : full // 2], d[:, full // 2 :]], axis=0)

    mine, other = pack(core), pack(1 - core)
    mine, tok = lax.optimization_barrier((mine, tok))
    fwd, bwd, yy, swap = along_x(1), along_x(-1), route(along_y), route(other_core)
    go = lambda x, pairs: lax.ppermute(x, BOTH, pairs)
    a, b, y = go(mine, fwd), go(mine, bwd), go(mine, yy)
    aa, ya, yb = go(a, fwd), go(a, yy), go(b, yy)
    yaa = go(aa, yy)
    got = [y, a, b, ya, yb, aa, yaa]
    packs = [mine, other] + got + [go(g, swap) for g in got]

    f1 = pl.pallas_call(
        first_kernel,
        out_shape=jax.ShapeDtypeStruct((n_seq, n_chan, r_own, own), BF),
        in_specs=[smem] + [vmem] * 3,
        out_specs=vmem,
        compiler_params=pltpu.CompilerParams(vmem_limit_bytes=32 << 20),
        name="first",
    )(place, tok, right_in, twiddle_in)
    col = lax.all_to_all(f1.reshape(n_seq * n_chan, r_own, own), BOTH, 0, 0, tiled=True)
    f3 = pl.pallas_call(
        middle_kernel,
        out_shape=jax.ShapeDtypeStruct((blocks, r_own, own), BF),
        in_specs=[vmem] * 5,
        out_specs=vmem,
        scratch_shapes=[pltpu.VMEM((blocks * r_own, own), F32)] * 2,
        compiler_params=pltpu.CompilerParams(vmem_limit_bytes=32 << 20),
        name="middle",
    )(col, left_in, left_out, kernel, gain_in[None])
    back = lax.all_to_all(f3, BOTH, 0, 0, tiled=True).reshape(n_seq, n_chan, r_own, own)
    count = len(packs)


    done = pl.pallas_call(
        functools.partial(last_kernel, count),
        out_shape=jax.ShapeDtypeStruct((n_chan, inner, own), BF),
        in_specs=[smem] + [vmem] * 5 + [any_] * count,
        out_specs=vmem,
        scratch_shapes=[
            pltpu.VMEM((count,) + mine.shape, BF),
            pltpu.VMEM((inner, full), F32),
            pltpu.VMEM((inner, full), BF),
            pltpu.SemaphoreType.DMA((count,)),
        ],
        compiler_params=pltpu.CompilerParams(vmem_limit_bytes=56 << 20),
        name="last",
    )(place, back, tok, right_out, twiddle_out, gain_mlp[None], *packs)
    out = lax.all_to_all(done, "chan", 0, 0, tiled=True)
    return out.reshape(tokens.shape)


def solution(mesh):
    in_specs = (
        P("seq", "chan"),
        P("chan"),
        P(),
        P("seq", None),
        P(),
        P(None, "seq", "chan"),
        P(),
        P(),
        P("seq", None),
        P(),
        P(None, "chan"),
        P(None, "chan"),
        P("chan", None),
    )
    return jax.shard_map(local, mesh=mesh, in_specs=in_specs, out_specs=P("seq", "chan"), check_vma=False)
```

```python
import functools

import jax
import jax.numpy as jnp
from jax import lax
from jax.experimental import pallas as pl
from jax.experimental.pallas import tpu as pltpu
from jax.sharding import PartitionSpec as P

EPS = 1e-06
BOTH = ("seq", "chan")
Z, CORE, YLO, X = 8, 2, 2, 4
YHI = 2
BF, F32 = jnp.bfloat16, jnp.float32


def route(move):
    pairs = []
    for yhi in range(YHI):
        for z in range(Z):
            for core in range(CORE):
                for ylo in range(YLO):
                    for x in range(X):
                        a, b, c, d, e = move(yhi, z, core, ylo, x)
                        src = (((yhi * Z + z) * CORE + core) * YLO + ylo) * X + x
                        dst = (((a * Z + b) * CORE + c) * YLO + d) * X + e
                        pairs.append((src, dst))
    return pairs


def along_x(sign):
    def move(yhi, z, core, ylo, x):
        step = sign if core == 0 else -sign
        return yhi, z, core, ylo, (x + step) % X

    return route(move)


def along_y(yhi, z, core, ylo, x):
    y = (yhi * YLO + ylo + (1 if core == 0 else -1)) % (YHI * YLO)
    return y // YLO, z, core, y % YLO, x


def other_core(yhi, z, core, ylo, x):
    return yhi, z, 1 - core, ylo, x


def touch_kernel(count, *rest):
    rest[count][...] = jnp.zeros_like(rest[count])


def touch(arrays, flops):
    return pl.pallas_call(
        functools.partial(touch_kernel, len(arrays)),
        out_shape=jax.ShapeDtypeStruct((8, 128), F32),
        in_specs=[pl.BlockSpec(memory_space=pl.ANY)] * len(arrays),
        out_specs=pl.BlockSpec(memory_space=pltpu.VMEM),
        cost_estimate=pl.CostEstimate(flops=flops, bytes_accessed=1, transcendentals=0),
        name="touch",
    )(*arrays)


def first_kernel(place, tok, right, tw, out):
    groups, rows, width = tok.shape
    energy = jnp.zeros((rows, 1), F32)
    for g in range(groups):
        t = tok[g].astype(F32)
        energy = energy + jnp.sum(t * t, axis=1, keepdims=True)
    scale = lax.rsqrt(energy / (groups * width) + EPS)
    turned = tw[...].T
    lane = lax.broadcasted_iota(jnp.int32, turned.shape, 1)
    twiddle = jnp.sum(jnp.where(lane == place[0], turned, 0.0), axis=1, keepdims=True)
    for g in range(0, groups, 2):
        pair = [(tok[g + k].astype(F32) * scale).astype(BF) for k in range(2)]
        f = jnp.dot(right[...], jnp.concatenate(pair, axis=1), preferred_element_type=F32)
        f = (f * twiddle).astype(BF)
        for k in range(2):
            part = f[:, k * width : (k + 1) * width]
            out[:, g + k] = part.reshape(out.shape[0], out.shape[2], width)


def middle_kernel(col, left_in, left_out, kern, gain, out, flat, kflat):
    blocks, inner, width = col.shape
    flat[...] = col[...].astype(F32).reshape(blocks * inner, width)
    kflat[...] = (kern[...].astype(F32) * gain[...][None]).reshape(blocks * inner, width)
    for r in range(0, inner, 2):
        at = [pl.ds(r + k, blocks, stride=inner) for k in range(2)]
        x = jnp.concatenate([flat[a, :].astype(BF) for a in at], axis=1)
        k = jnp.concatenate([kflat[a, :] for a in at], axis=1)
        two = jnp.dot(left_in[...], x, preferred_element_type=F32)
        two = (two * k).astype(BF)
        three = jnp.dot(left_out[...], two, preferred_element_type=F32)
        for i, a in enumerate(at):
            flat[a, :] = three[:, i * width : (i + 1) * width]
    out[...] = flat[...].reshape(blocks, inner, width).astype(BF)


def mlp_over(packs, weights, sems, first, second, normed, acc, prepare):
    full = normed.shape[1]
    hid, half = weights.shape[2] // 2, full // 2
    count, tall = weights.shape[:2]
    rows = packs[0].shape[1]
    per = tall // rows
    copies = []
    for pack in packs:
        for k in range(pack.shape[0]):
            i = len(copies)
            place = weights.at[i // per, pl.ds(i % per * rows, rows)]
            copies.append(pltpu.make_async_copy(pack.at[k], place, sems.at[i]))
            copies[i].start()
    prepare()

    def up_to(i, to):
        for copy in copies[i * per : (i + 1) * per]:
            copy.wait()
        to[...] = jnp.dot(normed[...], weights[i, :full, :], preferred_element_type=F32)

    def down_from(i, both):
        gate, up = both[:, :hid], both[:, hid:]
        hidden = (gate * up / (1.0 + jnp.exp(-gate))).astype(BF)
        for k in range(2):
            down = weights[i, full + k * hid : full + (k + 1) * hid, :]
            acc[:, k * half : (k + 1) * half] += jnp.dot(hidden, down, preferred_element_type=F32)

    held = (first, second)
    up_to(0, first)
    for i in range(count):
        if i + 1 < count:
            up_to(i + 1, held[(i + 1) % 2])
        down_from(i, held[i % 2])


def third_kernel(count, place, back, tok, right_hbm, tw, gain, *rest):
    packs, (acc, normed, right, sem, weights, sems, one, two) = rest[:count], rest[count:]
    load = pltpu.make_async_copy(right_hbm, right, sem)
    load.start()

    def prepare():
        groups, rows, width = tok.shape
        turned = tw[...].T
        lane = lax.broadcasted_iota(jnp.int32, turned.shape, 1)
        twiddle = jnp.sum(jnp.where(lane == place[0], turned, 0.0), axis=1, keepdims=True)
        energy = jnp.zeros((rows, 1), F32)
        load.wait()
        for g in range(0, groups, 2):
            pair = [back[:, g + k].reshape(rows, width) for k in range(2)]
            mixed = jnp.dot(right[...], jnp.concatenate(pair, axis=1), preferred_element_type=F32)
            mixed = mixed * twiddle
            for k in range(2):
                at = pl.ds((g + k) * width, width)
                s = tok[g + k].astype(F32) + mixed[:, k * width : (k + 1) * width]
                s = s.astype(BF).astype(F32)
                acc[:, at] = s
                energy = energy + jnp.sum(s * s, axis=1, keepdims=True)
        scale = lax.rsqrt(energy / (groups * width) + EPS)
        normed[...] = (acc[...] * scale * gain[...]).astype(BF)

    mlp_over(packs, weights, sems, one, two, normed, acc, prepare)


def more_kernel(count, before, normed, *rest):
    packs, (acc, weights, sems, one, two) = rest[:count], rest[count:]

    def prepare():
        acc[...] = before[...]

    mlp_over(packs, weights, sems, one, two, normed, acc, prepare)


def last_kernel(count, before, normed, *rest):
    packs, (out, acc, weights, sems, one, two) = rest[:count], rest[count:]

    def prepare():
        acc[...] = before[...]

    mlp_over(packs, weights, sems, one, two, normed, acc, prepare)
    groups, _, width = out.shape
    for g in range(groups):
        out[g] = acc[:, g * width : (g + 1) * width].astype(BF)


def local(tokens, gain_in, right_in, twiddle_in, left_in, kernel, left_out, right_out, twiddle_out, gain_mlp, w_gate, w_up, w_down):
    own = tokens.shape[1]
    inner = right_in.shape[0]
    n_chan = lax.axis_size("chan")
    n_seq = lax.axis_size("seq")
    blocks = left_in.shape[0]
    full = own * n_chan
    r_own = kernel.shape[1]
    hid = w_gate.shape[1] // 2
    place = lax.axis_index("chan").astype(jnp.int32)[None]
    core = lax.axis_index("seq") % CORE

    vmem = pl.BlockSpec(memory_space=pltpu.VMEM)
    smem = pl.BlockSpec(memory_space=pltpu.SMEM)
    any_ = pl.BlockSpec(memory_space=pl.ANY)
    hbm = pl.BlockSpec(memory_space=pltpu.HBM)

    tok = lax.all_to_all(tokens.reshape(n_chan, inner, own), "chan", 0, 0, tiled=True)

    halves = []
    for k in range(2):
        cut = slice(k * hid, (k + 1) * hid)
        d = w_down[cut]
        gate_up = jnp.concatenate([w_gate[:, cut], w_up[:, cut]], axis=1)
        halves.append(jnp.concatenate([gate_up, d[:, : full // 2], d[:, full // 2 :]], axis=0))
    mine = jnp.stack(halves)
    half = lambda w: lax.dynamic_slice_in_dim(w, core, 1, 0)
    fwd, yy, swap = along_x(1), route(along_y), route(other_core)
    go = lambda x, pairs: lax.ppermute(x, BOTH, pairs)
    mine, tok = lax.optimization_barrier((mine, tok))
    ab, y = go(mine, fwd), go(half(mine), yy)

    f1 = pl.pallas_call(
        first_kernel,
        out_shape=jax.ShapeDtypeStruct((n_seq, n_chan, r_own, own), BF),
        in_specs=[smem] + [vmem] * 3,
        out_specs=vmem,
        compiler_params=pltpu.CompilerParams(vmem_limit_bytes=60 << 20),
        cost_estimate=pl.CostEstimate(flops=1, bytes_accessed=1, transcendentals=0),
        name="first",
    )(place, tok, right_in, twiddle_in)
    col = lax.all_to_all(f1.reshape(n_seq * n_chan, r_own, own), BOTH, 0, 0, tiled=True)
    ab, y, col = lax.optimization_barrier((ab, y, col))
    cut = mine.shape[1] // 2
    quarter = lambda w, k: lax.dynamic_slice(w, (core, k * cut, 0), (1, cut, w.shape[2]))
    yab, a0, a1 = go(ab, yy), go(quarter(ab, 0), fwd), go(quarter(ab, 1), fwd)
    f3 = pl.pallas_call(
        middle_kernel,
        out_shape=jax.ShapeDtypeStruct((blocks, r_own, own), BF),
        in_specs=[vmem] * 5,
        out_specs=vmem,
        scratch_shapes=[pltpu.VMEM((blocks * r_own, own), F32)] * 2,
        compiler_params=pltpu.CompilerParams(vmem_limit_bytes=60 << 20),
        cost_estimate=pl.CostEstimate(flops=1, bytes_accessed=1, transcendentals=0),
        name="middle",
    )(col, left_in, left_out, kernel, gain_in[None])
    back = lax.all_to_all(f3, BOTH, 0, 0, tiled=True).reshape(n_seq, n_chan, r_own, own)
    back, mark = lax.optimization_barrier((back, touch([yab, a0, a1], 10**11)))
    yab, a0, a1, _ = lax.optimization_barrier((yab, a0, a1, mark))
    ya0, ya1 = go(a0, yy), go(quarter(yab, 1), fwd)
    both = lambda g: [g, go(g, swap)]
    shape = (inner, full)
    rows_f32, rows_bf = jax.ShapeDtypeStruct(shape, F32), jax.ShapeDtypeStruct(shape, BF)

    def mlp(body, name, inputs, specs, packs, outs, scratch):
        pieces = sum(p.shape[0] for p in packs)
        count = pieces * packs[0].shape[1] // mine.shape[1]
        return pl.pallas_call(
            functools.partial(body, len(packs)),
            out_shape=outs,
            in_specs=specs + [any_] * len(packs),
            out_specs=jax.tree.map(lambda _: vmem, outs),
            scratch_shapes=scratch
            + [
                pltpu.VMEM((count,) + mine.shape[1:], BF),
                pltpu.SemaphoreType.DMA((pieces,)),
                pltpu.VMEM((inner, 2 * hid), F32),
                pltpu.VMEM((inner, 2 * hid), F32),
            ],
            compiler_params=pltpu.CompilerParams(vmem_limit_bytes=32 << 20),
            cost_estimate=pl.CostEstimate(flops=10**11, bytes_accessed=1, transcendentals=0),
            name=name,
        )(*inputs, *packs)

    start = [place, back, tok, right_out, twiddle_out, gain_mlp[None]]
    extra = [pltpu.VMEM(right_out.shape, BF), pltpu.SemaphoreType.DMA]
    acc, normed = mlp(third_kernel, "third", start, [smem, vmem, vmem, hbm, vmem, vmem], [mine] + both(ab) + both(y), (rows_f32, rows_bf), extra)
    acc = mlp(more_kernel, "more", [acc, normed], [vmem] * 2, both(yab), rows_f32, [])
    done = jax.ShapeDtypeStruct((n_chan, inner, own), BF)
    done = mlp(last_kernel, "last", [acc, normed], [vmem] * 2, [a0, a1, go(a0, swap), go(a1, swap), ya0, ya1, go(ya0, swap), go(ya1, swap)], done, [pltpu.VMEM(shape, F32)])
    out = lax.all_to_all(done, "chan", 0, 0, tiled=True)
    return out.reshape(tokens.shape)


def solution(mesh):
    in_specs = (
        P("seq", "chan"),
        P("chan"),
        P(),
        P("seq", None),
        P(),
        P(None, "seq", "chan"),
        P(),
        P(),
        P("seq", None),
        P(),
        P(None, "chan"),
        P(None, "chan"),
        P("chan", None),
    )
    return jax.shard_map(local, mesh=mesh, in_specs=in_specs, out_specs=P("seq", "chan"), check_vma=False)
```

```python
import functools

import jax
import jax.numpy as jnp
from jax import lax
from jax.experimental import pallas as pl
from jax.experimental.pallas import tpu as pltpu
from jax.sharding import PartitionSpec as P

EPS = 1e-06
BOTH = ("seq", "chan")
Z, CORE, YLO, X = 8, 2, 2, 4
YHI = 2
BF, F32 = jnp.bfloat16, jnp.float32


def route(move):
    pairs = []
    for yhi in range(YHI):
        for z in range(Z):
            for core in range(CORE):
                for ylo in range(YLO):
                    for x in range(X):
                        a, b, c, d, e = move(yhi, z, core, ylo, x)
                        src = (((yhi * Z + z) * CORE + core) * YLO + ylo) * X + x
                        dst = (((a * Z + b) * CORE + c) * YLO + d) * X + e
                        pairs.append((src, dst))
    return pairs


def along_x(sign):
    def move(yhi, z, core, ylo, x):
        step = sign if core == 0 else -sign
        return yhi, z, core, ylo, (x + step) % X

    return route(move)


def along_y(yhi, z, core, ylo, x):
    y = (yhi * YLO + ylo + (1 if core == 0 else -1)) % (YHI * YLO)
    return y // YLO, z, core, y % YLO, x


def other_core(yhi, z, core, ylo, x):
    return yhi, z, 1 - core, ylo, x


def first_kernel(place, tok, right, tw, out):
    groups, rows, width = tok.shape
    energy = jnp.zeros((rows, 1), F32)
    for g in range(groups):
        t = tok[g].astype(F32)
        energy = energy + jnp.sum(t * t, axis=1, keepdims=True)
    scale = lax.rsqrt(energy / (groups * width) + EPS)
    turned = tw[...].T
    lane = lax.broadcasted_iota(jnp.int32, turned.shape, 1)
    twiddle = jnp.sum(jnp.where(lane == place[0], turned, 0.0), axis=1, keepdims=True)
    for g in range(0, groups, 2):
        pair = [(tok[g + k].astype(F32) * scale).astype(BF) for k in range(2)]
        f = jnp.dot(right[...], jnp.concatenate(pair, axis=1), preferred_element_type=F32)
        f = (f * twiddle).astype(BF)
        for k in range(2):
            part = f[:, k * width : (k + 1) * width]
            out[:, g + k] = part.reshape(out.shape[0], out.shape[2], width)


def middle_kernel(col, left_in, left_out, kern, gain, out, flat, kflat):
    blocks, inner, width = col.shape
    flat[...] = col[...].astype(F32).reshape(blocks * inner, width)
    kflat[...] = (kern[...].astype(F32) * gain[...][None]).reshape(blocks * inner, width)
    for r in range(0, inner, 2):
        at = [pl.ds(r + k, blocks, stride=inner) for k in range(2)]
        x = jnp.concatenate([flat[a, :].astype(BF) for a in at], axis=1)
        k = jnp.concatenate([kflat[a, :] for a in at], axis=1)
        two = jnp.dot(left_in[...], x, preferred_element_type=F32)
        two = (two * k).astype(BF)
        three = jnp.dot(left_out[...], two, preferred_element_type=F32)
        for i, a in enumerate(at):
            flat[a, :] = three[:, i * width : (i + 1) * width]
    out[...] = flat[...].reshape(blocks, inner, width).astype(BF)


def mlp_over(packs, weights, sems, first, second, normed, acc, prepare):
    full = normed.shape[1]
    hid, half = weights.shape[2] // 2, full // 2
    count = weights.shape[0]
    slots = [[] for _ in range(count)]
    at = 0
    tall = weights.shape[1]
    for pack, (done, stop) in packs:
        while done < stop:
            i, row = at // tall, at % tall
            rows = min(stop - done, tall - row)
            sem = sems.at[sum(map(len, slots))]
            piece = pack.at[0, pl.ds(done, rows)]
            slots[i].append(pltpu.make_async_copy(piece, weights.at[i, pl.ds(row, rows)], sem))
            slots[i][-1].start()
            at, done = at + rows, done + rows
    prepare()

    def up_to(i, to):
        for copy in slots[i]:
            copy.wait()
        to[...] = jnp.dot(normed[...], weights[i, :full, :], preferred_element_type=F32)

    def down_from(i, both):
        gate, up = both[:, :hid], both[:, hid:]
        hidden = (gate * up / (1.0 + jnp.exp(-gate))).astype(BF)
        for k in range(2):
            down = weights[i, full + k * hid : full + (k + 1) * hid, :]
            acc[:, k * half : (k + 1) * half] += jnp.dot(hidden, down, preferred_element_type=F32)

    held = (first, second)
    up_to(0, first)
    for i in range(count):
        if i + 1 < count:
            up_to(i + 1, held[(i + 1) % 2])
        down_from(i, held[i % 2])


def third_kernel(place, back, tok, right_hbm, tw, gain, stream, normed, acc, right, sem):
    load = pltpu.make_async_copy(right_hbm, right, sem)
    load.start()
    groups, rows, width = tok.shape
    turned = tw[...].T
    lane = lax.broadcasted_iota(jnp.int32, turned.shape, 1)
    twiddle = jnp.sum(jnp.where(lane == place[0], turned, 0.0), axis=1, keepdims=True)
    energy = jnp.zeros((rows, 1), F32)
    load.wait()
    for g in range(0, groups, 2):
        pair = [back[:, g + k].reshape(rows, width) for k in range(2)]
        mixed = jnp.dot(right[...], jnp.concatenate(pair, axis=1), preferred_element_type=F32)
        mixed = mixed * twiddle
        for k in range(2):
            at = pl.ds((g + k) * width, width)
            s = tok[g + k].astype(F32) + mixed[:, k * width : (k + 1) * width]
            stream[:, at] = s.astype(BF)
            s = s.astype(BF).astype(F32)
            acc[:, at] = s
            energy = energy + jnp.sum(s * s, axis=1, keepdims=True)
    scale = lax.rsqrt(energy / (groups * width) + EPS)
    normed[...] = (acc[...] * scale * gain[...]).astype(BF)


def mlp_kernel(spans, begun, normed, before, *rest):
    packs, (out, *spare, weights, sems, one, two) = rest[: len(spans)], rest[len(spans) :]
    packs = list(zip(packs, spans))
    acc = spare[0] if spare else out

    def prepare():
        acc[...] = before[...].astype(F32) if begun else jnp.zeros_like(acc)

    mlp_over(packs, weights, sems, one, two, normed, acc, prepare)
    if spare:
        out[...] = acc[...].astype(out.dtype)


def sum_kernel(a, b, out):
    groups, _, width = out.shape
    for g in range(groups):
        at = slice(g * width, (g + 1) * width)
        out[g] = (a[:, at].astype(F32) + b[:, at].astype(F32)).astype(BF)


def local(tokens, gain_in, right_in, twiddle_in, left_in, kernel, left_out, right_out, twiddle_out, gain_mlp, w_gate, w_up, w_down):
    own = tokens.shape[1]
    inner = right_in.shape[0]
    n_chan = lax.axis_size("chan")
    n_seq = lax.axis_size("seq")
    blocks = left_in.shape[0]
    full = own * n_chan
    r_own = kernel.shape[1]
    hid = w_gate.shape[1] // 2
    place = lax.axis_index("chan").astype(jnp.int32)[None]
    core = lax.axis_index("seq") % CORE

    vmem = pl.BlockSpec(memory_space=pltpu.VMEM)
    smem = pl.BlockSpec(memory_space=pltpu.SMEM)
    any_ = pl.BlockSpec(memory_space=pl.ANY)
    hbm = pl.BlockSpec(memory_space=pltpu.HBM)

    tok = lax.all_to_all(tokens.reshape(n_chan, inner, own), "chan", 0, 0, tiled=True)

    def pack(side):
        cut = lambda w, axis: lax.dynamic_slice_in_dim(w, side * hid, hid, axis)
        d = cut(w_down, 0)
        up = jnp.concatenate([cut(w_gate, 1), cut(w_up, 1)], axis=1)
        return jnp.concatenate([up, d[:, : full // 2], d[:, full // 2 :]], axis=0)

    own_half, other_half = pack(core), pack(1 - core)
    tall = own_half.shape[0]
    cut = tall // 2
    most = jnp.concatenate([other_half, own_half[:cut]])[None]
    q0, q1 = own_half[None, :cut], own_half[None, cut:]
    most, q0, q1, tok = lax.optimization_barrier((most, q0, q1, tok))
    fwd, yy, swap = along_x(1), route(along_y), route(other_core)
    go = lambda x, pairs: lax.ppermute(x, BOTH, pairs)
    a_most, a1, y0, y1 = go(most, fwd), go(q1, fwd), go(q0, yy), go(q1, yy)

    f1 = pl.pallas_call(
        first_kernel,
        out_shape=jax.ShapeDtypeStruct((n_seq, n_chan, r_own, own), BF),
        in_specs=[smem] + [vmem] * 3,
        out_specs=vmem,
        compiler_params=pltpu.CompilerParams(vmem_limit_bytes=60 << 20),
        cost_estimate=pl.CostEstimate(flops=1, bytes_accessed=1, transcendentals=0),
        name="first",
    )(place, tok, right_in, twiddle_in)
    col = lax.all_to_all(f1.reshape(n_seq * n_chan, r_own, own), BOTH, 0, 0, tiled=True)
    a_most, a1, y0, y1, col = lax.optimization_barrier((a_most, a1, y0, y1, col))
    ya_most, ay1 = go(a_most, yy), go(y1, fwd)
    aa0, aa1 = go(a_most[:, tall:], fwd), go(a1, fwd)
    f3 = pl.pallas_call(
        middle_kernel,
        out_shape=jax.ShapeDtypeStruct((blocks, r_own, own), BF),
        in_specs=[vmem] * 5,
        out_specs=vmem,
        scratch_shapes=[pltpu.VMEM((blocks * r_own, own), F32)] * 2,
        compiler_params=pltpu.CompilerParams(vmem_limit_bytes=44 << 20),
        cost_estimate=pl.CostEstimate(flops=1, bytes_accessed=1, transcendentals=0),
        name="middle",
    )(col, left_in, left_out, kernel, gain_in[None])
    back = lax.all_to_all(f3, BOTH, 0, 0, tiled=True).reshape(n_seq, n_chan, r_own, own)
    late = [go(aa0, yy), go(ay1, fwd)]
    shape = (inner, full)
    rows_f32, rows_bf = jax.ShapeDtypeStruct(shape, F32), jax.ShapeDtypeStruct(shape, BF)
    room = pltpu.CompilerParams(vmem_limit_bytes=28 << 20)
    cost = pl.CostEstimate(flops=10**11, bytes_accessed=1, transcendentals=0)
    stream, normed = pl.pallas_call(
        third_kernel,
        out_shape=(rows_bf, rows_bf),
        in_specs=[smem, vmem, vmem, any_, vmem, vmem],
        out_specs=(vmem, vmem),
        scratch_shapes=[pltpu.VMEM(shape, F32), pltpu.VMEM(right_out.shape, BF), pltpu.SemaphoreType.DMA],
        compiler_params=room,
        name="third",
    )(place, back, tok, right_out, twiddle_out, gain_mlp[None])

    def mlp(name, rows, before, begun, packs, out):
        packs, spans = zip(*packs)
        count = sum(stop - start for start, stop in spans) // tall
        pieces = sum(-(-(stop - start) // tall) for start, stop in spans)
        return pl.pallas_call(
            functools.partial(mlp_kernel, spans, begun),
            out_shape=out,
            in_specs=[vmem, vmem if begun else any_] + [any_] * len(packs),
            out_specs=vmem,
            scratch_shapes=([] if out is rows_f32 else [pltpu.VMEM(shape, F32)])
            + [
                pltpu.VMEM((count, tall, 2 * hid), BF),
                pltpu.SemaphoreType.DMA((pieces,)),
                pltpu.VMEM((inner, 2 * hid), F32),
                pltpu.VMEM((inner, 2 * hid), F32),
            ],
            compiler_params=room,
            cost_estimate=cost,
            name=name,
        )(rows, before, *packs)

    theirs = go(normed, swap)
    whole = lambda *arrays: [(w, (0, w.shape[1])) for w in arrays]
    early = whole(q0, q1, a_most, a1, y0, y1) + [(ya_most, (0, tall))]
    late = [(ya_most, (tall, tall + cut))] + whole(ay1, aa0, aa1, *late)
    own_sum = mlp("own", normed, stream, True, early, rows_f32)
    their_sum = mlp("their", theirs, own_sum, False, early, rows_f32)
    partial = go(mlp("their_late", theirs, their_sum, True, late, rows_bf), swap)
    own_sum = mlp("own_late", normed, own_sum, True, late, rows_f32)
    done = pl.pallas_call(
        sum_kernel,
        out_shape=jax.ShapeDtypeStruct((n_chan, inner, own), BF),
        in_specs=[vmem] * 2,
        out_specs=vmem,
        compiler_params=room,
        name="sum",
    )(own_sum, partial)
    out = lax.all_to_all(done, "chan", 0, 0, tiled=True)
    return out.reshape(tokens.shape)


def solution(mesh):
    in_specs = (
        P("seq", "chan"),
        P("chan"),
        P(),
        P("seq", None),
        P(),
        P(None, "seq", "chan"),
        P(),
        P(),
        P("seq", None),
        P(),
        P(None, "chan"),
        P(None, "chan"),
        P("chan", None),
    )
    return jax.shard_map(local, mesh=mesh, in_specs=in_specs, out_specs=P("seq", "chan"), check_vma=False)
```

```python
import functools

import jax
import jax.numpy as jnp
from jax import lax
from jax.experimental import pallas as pl
from jax.experimental.pallas import tpu as pltpu
from jax.sharding import PartitionSpec as P

EPS = 1e-06
BOTH = ("seq", "chan")
Z, CORE, YLO, X = 8, 2, 2, 4
YHI = 2
BF, F32 = jnp.bfloat16, jnp.float32


def route(move):
    pairs = []
    for yhi in range(YHI):
        for z in range(Z):
            for core in range(CORE):
                for ylo in range(YLO):
                    for x in range(X):
                        a, b, c, d, e = move(yhi, z, core, ylo, x)
                        src = (((yhi * Z + z) * CORE + core) * YLO + ylo) * X + x
                        dst = (((a * Z + b) * CORE + c) * YLO + d) * X + e
                        pairs.append((src, dst))
    return pairs


def along_x(sign):
    def move(yhi, z, core, ylo, x):
        step = sign if core == 0 else -sign
        return yhi, z, core, ylo, (x + step) % X

    return route(move)


def along_y(yhi, z, core, ylo, x):
    y = (yhi * YLO + ylo + (1 if core == 0 else -1)) % (YHI * YLO)
    return y // YLO, z, core, y % YLO, x


def other_core(yhi, z, core, ylo, x):
    return yhi, z, 1 - core, ylo, x


def first_kernel(place, tok, right, tw, out):
    groups, rows, width = tok.shape
    energy = jnp.zeros((rows, 1), F32)
    for g in range(groups):
        t = tok[g].astype(F32)
        energy = energy + jnp.sum(t * t, axis=1, keepdims=True)
    scale = lax.rsqrt(energy / (groups * width) + EPS)
    turned = tw[...].T
    lane = lax.broadcasted_iota(jnp.int32, turned.shape, 1)
    twiddle = jnp.sum(jnp.where(lane == place[0], turned, 0.0), axis=1, keepdims=True)
    for g in range(0, groups, 2):
        pair = [(tok[g + k].astype(F32) * scale).astype(BF) for k in range(2)]
        f = jnp.dot(right[...], jnp.concatenate(pair, axis=1), preferred_element_type=F32)
        f = (f * twiddle).astype(BF)
        for k in range(2):
            part = f[:, k * width : (k + 1) * width]
            out[:, g + k] = part.reshape(out.shape[0], out.shape[2], width)


def middle_kernel(col, left_in, left_out, kern, gain, out, flat, kflat):
    blocks, inner, width = col.shape
    flat[...] = col[...].astype(F32).reshape(blocks * inner, width)
    kflat[...] = (kern[...].astype(F32) * gain[...][None]).reshape(blocks * inner, width)
    for r in range(0, inner, 2):
        at = [pl.ds(r + k, blocks, stride=inner) for k in range(2)]
        x = jnp.concatenate([flat[a, :].astype(BF) for a in at], axis=1)
        k = jnp.concatenate([kflat[a, :] for a in at], axis=1)
        two = jnp.dot(left_in[...], x, preferred_element_type=F32)
        two = (two * k).astype(BF)
        three = jnp.dot(left_out[...], two, preferred_element_type=F32)
        for i, a in enumerate(at):
            flat[a, :] = three[:, i * width : (i + 1) * width]
    out[...] = flat[...].reshape(blocks, inner, width).astype(BF)


def mlp_over(packs, weights, sems, first, second, normed, acc, base):
    full = normed.shape[1]
    hid, half = weights.shape[2] // 2, full // 2
    count = weights.shape[0]
    slots = [[] for _ in range(count)]
    at = 0
    tall = weights.shape[1]
    for pack, (done, stop) in packs:
        while done < stop:
            i, row = at // tall, at % tall
            rows = min(stop - done, tall - row)
            sem = sems.at[sum(map(len, slots))]
            piece = pack.at[0, pl.ds(done, rows)]
            slots[i].append(pltpu.make_async_copy(piece, weights.at[i, pl.ds(row, rows)], sem))
            at, done = at + rows, done + rows
    for i in range(min(2, count)):
        for copy in slots[i]:
            copy.start()

    def up_to(i, to):
        for copy in slots[i]:
            copy.wait()
        if i + 2 < count:
            for copy in slots[i + 2]:
                copy.start()
        to[...] = jnp.dot(normed[...], weights[i, :full, :], preferred_element_type=F32)

    def down_from(i, both):
        gate, up = both[:, :hid], both[:, hid:]
        hidden = (gate * up / (1.0 + jnp.exp(-gate))).astype(BF)
        for k in range(2):
            down = weights[i, full + k * hid : full + (k + 1) * hid, :]
            at = slice(k * half, (k + 1) * half)
            part = jnp.dot(hidden, down, preferred_element_type=F32)
            if i > 0:
                part = part + acc[:, at]
            elif base is not None:
                part = part + base[:, at].astype(F32)
            acc[:, at] = part

    held = (first, second)
    up_to(0, first)
    for i in range(count):
        if i + 1 < count:
            up_to(i + 1, held[(i + 1) % 2])
        down_from(i, held[i % 2])


def third_kernel(place, back, tok, right_hbm, tw, gain, stream, normed, acc, right, sem):
    load = pltpu.make_async_copy(right_hbm, right, sem)
    load.start()
    groups, rows, width = tok.shape
    turned = tw[...].T
    lane = lax.broadcasted_iota(jnp.int32, turned.shape, 1)
    twiddle = jnp.sum(jnp.where(lane == place[0], turned, 0.0), axis=1, keepdims=True)
    energy = jnp.zeros((rows, 1), F32)
    load.wait()
    for g in range(0, groups, 2):
        pair = [back[:, g + k].reshape(rows, width) for k in range(2)]
        mixed = jnp.dot(right[...], jnp.concatenate(pair, axis=1), preferred_element_type=F32)
        mixed = mixed * twiddle
        for k in range(2):
            at = pl.ds((g + k) * width, width)
            s = tok[g + k].astype(F32) + mixed[:, k * width : (k + 1) * width]
            stream[:, at] = s.astype(BF)
            s = s.astype(BF).astype(F32)
            acc[:, at] = s
            energy = energy + jnp.sum(s * s, axis=1, keepdims=True)
    scale = lax.rsqrt(energy / (groups * width) + EPS)
    normed[...] = (acc[...] * scale * gain[...]).astype(BF)


def mlp_kernel(spans, begun, normed, before, *rest):
    packs, (out, *spare, weights, sems, one, two) = rest[: len(spans)], rest[len(spans) :]
    packs = list(zip(packs, spans))
    acc = spare[0] if spare else out

    mlp_over(packs, weights, sems, one, two, normed, acc, before if begun else None)
    if spare:
        out[...] = acc[...].astype(out.dtype)


def sum_kernel(a, b, out):
    groups, _, width = out.shape
    for g in range(groups):
        at = slice(g * width, (g + 1) * width)
        out[g] = (a[:, at].astype(F32) + b[:, at].astype(F32)).astype(BF)


def local(tokens, gain_in, right_in, twiddle_in, left_in, kernel, left_out, right_out, twiddle_out, gain_mlp, w_gate, w_up, w_down):
    own = tokens.shape[1]
    inner = right_in.shape[0]
    n_chan = lax.axis_size("chan")
    n_seq = lax.axis_size("seq")
    blocks = left_in.shape[0]
    full = own * n_chan
    r_own = kernel.shape[1]
    hid = w_gate.shape[1] // 2
    place = lax.axis_index("chan").astype(jnp.int32)[None]
    core = lax.axis_index("seq") % CORE

    vmem = pl.BlockSpec(memory_space=pltpu.VMEM)
    smem = pl.BlockSpec(memory_space=pltpu.SMEM)
    any_ = pl.BlockSpec(memory_space=pl.ANY)
    hbm = pl.BlockSpec(memory_space=pltpu.HBM)

    tok = lax.all_to_all(tokens.reshape(n_chan, inner, own), "chan", 0, 0, tiled=True)

    def pack(side):
        cut = lambda w, axis: lax.dynamic_slice_in_dim(w, side * hid, hid, axis)
        d = cut(w_down, 0)
        up = jnp.concatenate([cut(w_gate, 1), cut(w_up, 1)], axis=1)
        return jnp.concatenate([up, d[:, : full // 2], d[:, full // 2 :]], axis=0)

    own_half, other_half = pack(core), pack(1 - core)
    tall = own_half.shape[0]
    cut = tall // 2
    most = jnp.concatenate([other_half, own_half[:cut]])[None]
    q0, q1 = own_half[None, :cut], own_half[None, cut:]
    most, q0, q1, tok = lax.optimization_barrier((most, q0, q1, tok))
    fwd, yy, swap = along_x(1), route(along_y), route(other_core)
    go = lambda x, pairs: lax.ppermute(x, BOTH, pairs)
    a_most, a1, y0, y1 = go(most, fwd), go(q1, fwd), go(q0, yy), go(q1, yy)

    f1 = pl.pallas_call(
        first_kernel,
        out_shape=jax.ShapeDtypeStruct((n_seq, n_chan, r_own, own), BF),
        in_specs=[smem] + [vmem] * 3,
        out_specs=vmem,
        compiler_params=pltpu.CompilerParams(vmem_limit_bytes=60 << 20),
        cost_estimate=pl.CostEstimate(flops=1, bytes_accessed=1, transcendentals=0),
        name="first",
    )(place, tok, right_in, twiddle_in)
    col = lax.all_to_all(f1.reshape(n_seq * n_chan, r_own, own), BOTH, 0, 0, tiled=True)
    a_most, a1, y0, y1, col = lax.optimization_barrier((a_most, a1, y0, y1, col))
    ya_most, ay1 = go(a_most, yy), go(y1, fwd)
    aa0, aa1 = go(a_most[:, tall:], fwd), go(a1, fwd)
    f3 = pl.pallas_call(
        middle_kernel,
        out_shape=jax.ShapeDtypeStruct((blocks, r_own, own), BF),
        in_specs=[vmem] * 5,
        out_specs=vmem,
        scratch_shapes=[pltpu.VMEM((blocks * r_own, own), F32)] * 2,
        compiler_params=pltpu.CompilerParams(vmem_limit_bytes=44 << 20),
        cost_estimate=pl.CostEstimate(flops=1, bytes_accessed=1, transcendentals=0),
        name="middle",
    )(col, left_in, left_out, kernel, gain_in[None])
    back = lax.all_to_all(f3, BOTH, 0, 0, tiled=True).reshape(n_seq, n_chan, r_own, own)
    late = [go(aa0, yy), go(ay1, fwd)]
    shape = (inner, full)
    rows_f32, rows_bf = jax.ShapeDtypeStruct(shape, F32), jax.ShapeDtypeStruct(shape, BF)
    room = pltpu.CompilerParams(vmem_limit_bytes=28 << 20)
    cost = pl.CostEstimate(flops=10**11, bytes_accessed=1, transcendentals=0)
    stream, normed = pl.pallas_call(
        third_kernel,
        out_shape=(rows_bf, rows_bf),
        in_specs=[smem, vmem, vmem, any_, vmem, vmem],
        out_specs=(vmem, vmem),
        scratch_shapes=[pltpu.VMEM(shape, F32), pltpu.VMEM(right_out.shape, BF), pltpu.SemaphoreType.DMA],
        compiler_params=room,
        name="third",
    )(place, back, tok, right_out, twiddle_out, gain_mlp[None])

    def mlp(name, rows, before, begun, packs, out):
        packs, spans = zip(*packs)
        count = sum(stop - start for start, stop in spans) // tall
        pieces = sum(-(-(stop - start) // tall) for start, stop in spans)
        return pl.pallas_call(
            functools.partial(mlp_kernel, spans, begun),
            out_shape=out,
            in_specs=[vmem, vmem if begun else any_] + [any_] * len(packs),
            out_specs=vmem,
            scratch_shapes=([] if out is rows_f32 else [pltpu.VMEM(shape, F32)])
            + [
                pltpu.VMEM((count, tall, 2 * hid), BF),
                pltpu.SemaphoreType.DMA((pieces,)),
                pltpu.VMEM((inner, 2 * hid), F32),
                pltpu.VMEM((inner, 2 * hid), F32),
            ],
            compiler_params=room,
            cost_estimate=cost,
            name=name,
        )(rows, before, *packs)

    theirs = go(normed, swap)
    whole = lambda *arrays: [(w, (0, w.shape[1])) for w in arrays]
    early = whole(q0, q1, a_most, a1, y0, y1, ya_most, ay1)
    late = whole(aa0, aa1, *late)
    own_sum = mlp("own", normed, stream, True, early, rows_f32)
    their_sum = mlp("their", theirs, own_sum, False, early, rows_f32)
    partial = go(mlp("their_late", theirs, their_sum, True, late, rows_bf), swap)
    own_sum = mlp("own_late", normed, own_sum, True, late, rows_f32)
    done = pl.pallas_call(
        sum_kernel,
        out_shape=jax.ShapeDtypeStruct((n_chan, inner, own), BF),
        in_specs=[vmem] * 2,
        out_specs=vmem,
        compiler_params=room,
        name="sum",
    )(own_sum, partial)
    out = lax.all_to_all(done, "chan", 0, 0, tiled=True)
    return out.reshape(tokens.shape)


def solution(mesh):
    in_specs = (
        P("seq", "chan"),
        P("chan"),
        P(),
        P("seq", None),
        P(),
        P(None, "seq", "chan"),
        P(),
        P(),
        P("seq", None),
        P(),
        P(None, "chan"),
        P(None, "chan"),
        P("chan", None),
    )
    return jax.shard_map(local, mesh=mesh, in_specs=in_specs, out_specs=P("seq", "chan"), check_vma=False)
```

```python
import functools

import jax
import jax.numpy as jnp
from jax import lax
from jax.experimental import pallas as pl
from jax.experimental.pallas import tpu as pltpu
from jax.sharding import PartitionSpec as P

EPS = 1e-06
BOTH = ("seq", "chan")
Z, CORE, YLO, X = 8, 2, 2, 4
YHI = 2
BF, F32 = jnp.bfloat16, jnp.float32


def route(move):
    pairs = []
    for yhi in range(YHI):
        for z in range(Z):
            for core in range(CORE):
                for ylo in range(YLO):
                    for x in range(X):
                        a, b, c, d, e = move(yhi, z, core, ylo, x)
                        src = (((yhi * Z + z) * CORE + core) * YLO + ylo) * X + x
                        dst = (((a * Z + b) * CORE + c) * YLO + d) * X + e
                        pairs.append((src, dst))
    return pairs


def along_x(sign):
    def move(yhi, z, core, ylo, x):
        step = sign if core == 0 else -sign
        return yhi, z, core, ylo, (x + step) % X

    return route(move)


def along_y(yhi, z, core, ylo, x):
    y = (yhi * YLO + ylo + (1 if core == 0 else -1)) % (YHI * YLO)
    return y // YLO, z, core, y % YLO, x


def other_core(yhi, z, core, ylo, x):
    return yhi, z, 1 - core, ylo, x


def first_kernel(place, tok, right, tw, out):
    groups, rows, width = tok.shape
    energy = jnp.zeros((rows, 1), F32)
    for g in range(groups):
        t = tok[g].astype(F32)
        energy = energy + jnp.sum(t * t, axis=1, keepdims=True)
    scale = lax.rsqrt(energy / (groups * width) + EPS)
    turned = tw[...].T
    lane = lax.broadcasted_iota(jnp.int32, turned.shape, 1)
    twiddle = jnp.sum(jnp.where(lane == place[0], turned, 0.0), axis=1, keepdims=True)
    for g in range(0, groups, 2):
        pair = [(tok[g + k].astype(F32) * scale).astype(BF) for k in range(2)]
        f = jnp.dot(right[...], jnp.concatenate(pair, axis=1), preferred_element_type=F32)
        f = (f * twiddle).astype(BF)
        for k in range(2):
            part = f[:, k * width : (k + 1) * width]
            out[:, g + k] = part.reshape(out.shape[0], out.shape[2], width)


def middle_kernel(col, left_in, left_out, kern, gain, out, flat, kflat):
    blocks, inner, width = col.shape
    flat[...] = col[...].astype(F32).reshape(blocks * inner, width)
    kflat[...] = (kern[...].astype(F32) * gain[...][None]).reshape(blocks * inner, width)
    for r in range(0, inner, 2):
        at = [pl.ds(r + k, blocks, stride=inner) for k in range(2)]
        x = jnp.concatenate([flat[a, :].astype(BF) for a in at], axis=1)
        k = jnp.concatenate([kflat[a, :] for a in at], axis=1)
        two = jnp.dot(left_in[...], x, preferred_element_type=F32)
        two = (two * k).astype(BF)
        three = jnp.dot(left_out[...], two, preferred_element_type=F32)
        for i, a in enumerate(at):
            flat[a, :] = three[:, i * width : (i + 1) * width]
    out[...] = flat[...].reshape(blocks, inner, width).astype(BF)


def mlp_over(packs, weights, sems, first, second, normed, acc, base):
    full = normed.shape[1]
    hid, half = weights.shape[2] // 2, full // 2
    count = weights.shape[0]
    slots = [[] for _ in range(count)]
    at = 0
    tall = weights.shape[1]
    for pack, (done, stop) in packs:
        while done < stop:
            i, row = at // tall, at % tall
            rows = min(stop - done, tall - row)
            sem = sems.at[sum(map(len, slots))]
            piece = pack.at[0, pl.ds(done, rows)]
            slots[i].append(pltpu.make_async_copy(piece, weights.at[i, pl.ds(row, rows)], sem))
            at, done = at + rows, done + rows
    for i in range(min(2, count)):
        for copy in slots[i]:
            copy.start()

    def up_to(i, to):
        for copy in slots[i]:
            copy.wait()
        if i + 2 < count:
            for copy in slots[i + 2]:
                copy.start()
        to[...] = jnp.dot(normed[...], weights[i, :full, :], preferred_element_type=F32)

    def down_from(i, both):
        gate, up = both[:, :hid], both[:, hid:]
        hidden = (gate * up / (1.0 + jnp.exp(-gate))).astype(BF)
        for k in range(2):
            down = weights[i, full + k * hid : full + (k + 1) * hid, :]
            at = slice(k * half, (k + 1) * half)
            part = jnp.dot(hidden, down, preferred_element_type=F32)
            if i > 0:
                part = part + acc[:, at]
            elif base is not None:
                part = part + base[:, at].astype(F32)
            acc[:, at] = part

    held = (first, second)
    up_to(0, first)
    for i in range(count):
        if i + 1 < count:
            up_to(i + 1, held[(i + 1) % 2])
        down_from(i, held[i % 2])


def third_kernel(place, back, tok, right_hbm, tw, gain, stream, normed, acc, right, sem):
    load = pltpu.make_async_copy(right_hbm, right, sem)
    load.start()
    groups, rows, width = tok.shape
    turned = tw[...].T
    lane = lax.broadcasted_iota(jnp.int32, turned.shape, 1)
    twiddle = jnp.sum(jnp.where(lane == place[0], turned, 0.0), axis=1, keepdims=True)
    energy = jnp.zeros((rows, 1), F32)
    load.wait()
    for g in range(0, groups, 2):
        pair = [back[:, g + k].reshape(rows, width) for k in range(2)]
        mixed = jnp.dot(right[...], jnp.concatenate(pair, axis=1), preferred_element_type=F32)
        mixed = mixed * twiddle
        for k in range(2):
            at = pl.ds((g + k) * width, width)
            s = tok[g + k].astype(F32) + mixed[:, k * width : (k + 1) * width]
            stream[:, at] = s.astype(BF)
            s = s.astype(BF).astype(F32)
            acc[:, at] = s
            energy = energy + jnp.sum(s * s, axis=1, keepdims=True)
    scale = lax.rsqrt(energy / (groups * width) + EPS)
    normed[...] = (acc[...] * scale * gain[...]).astype(BF)


def mlp_kernel(spans, begun, normed, before, *rest):
    packs, (out, *spare, weights, sems, one, two) = rest[: len(spans)], rest[len(spans) :]
    packs = list(zip(packs, spans))
    acc = spare[0] if spare else out

    mlp_over(packs, weights, sems, one, two, normed, acc, before if begun else None)
    if spare:
        out[...] = acc[...].astype(out.dtype)


def sum_kernel(a, b, out):
    groups, _, width = out.shape
    for g in range(groups):
        at = slice(g * width, (g + 1) * width)
        out[g] = (a[:, at].astype(F32) + b[:, at].astype(F32)).astype(BF)


def local(tokens, gain_in, right_in, twiddle_in, left_in, kernel, left_out, right_out, twiddle_out, gain_mlp, w_gate, w_up, w_down):
    own = tokens.shape[1]
    inner = right_in.shape[0]
    n_chan = lax.axis_size("chan")
    n_seq = lax.axis_size("seq")
    blocks = left_in.shape[0]
    full = own * n_chan
    r_own = kernel.shape[1]
    hid = w_gate.shape[1] // 2
    place = lax.axis_index("chan").astype(jnp.int32)[None]
    core = lax.axis_index("seq") % CORE

    vmem = pl.BlockSpec(memory_space=pltpu.VMEM)
    smem = pl.BlockSpec(memory_space=pltpu.SMEM)
    any_ = pl.BlockSpec(memory_space=pl.ANY)
    hbm = pl.BlockSpec(memory_space=pltpu.HBM)

    tok = lax.all_to_all(tokens.reshape(n_chan, inner, own), "chan", 0, 0, tiled=True)

    def pack(side):
        cut = lambda w, axis: lax.dynamic_slice_in_dim(w, side * hid, hid, axis)
        d = cut(w_down, 0)
        up = jnp.concatenate([cut(w_gate, 1), cut(w_up, 1)], axis=1)
        return jnp.concatenate([up, d[:, : full // 2], d[:, full // 2 :]], axis=0)

    own_half, other_half = pack(core), pack(1 - core)
    tall = own_half.shape[0]
    cut = tall // 2
    most = jnp.concatenate([other_half, own_half[:cut]])[None]
    q0, q1 = own_half[None, :cut], own_half[None, cut:]
    most, q0, q1, tok = lax.optimization_barrier((most, q0, q1, tok))
    fwd, yy, swap = along_x(1), route(along_y), route(other_core)
    go = lambda x, pairs: lax.ppermute(x, BOTH, pairs)
    a_most, a1, y0, y1 = go(most, fwd), go(q1, fwd), go(q0, yy), go(q1, yy)

    f1 = pl.pallas_call(
        first_kernel,
        out_shape=jax.ShapeDtypeStruct((n_seq, n_chan, r_own, own), BF),
        in_specs=[smem] + [vmem] * 3,
        out_specs=vmem,
        compiler_params=pltpu.CompilerParams(vmem_limit_bytes=60 << 20),
        cost_estimate=pl.CostEstimate(flops=1, bytes_accessed=1, transcendentals=0),
        name="first",
    )(place, tok, right_in, twiddle_in)
    col = lax.all_to_all(f1.reshape(n_seq * n_chan, r_own, own), BOTH, 0, 0, tiled=True)
    a_most, col = lax.optimization_barrier((a_most, col))
    ya_most, ay1 = go(a_most, yy), go(y1, fwd)
    aa0, aa1 = go(a_most[:, tall:], fwd), go(a1, fwd)
    f3 = pl.pallas_call(
        middle_kernel,
        out_shape=jax.ShapeDtypeStruct((blocks, r_own, own), BF),
        in_specs=[vmem] * 5,
        out_specs=vmem,
        scratch_shapes=[pltpu.VMEM((blocks * r_own, own), F32)] * 2,
        compiler_params=pltpu.CompilerParams(vmem_limit_bytes=44 << 20),
        cost_estimate=pl.CostEstimate(flops=1, bytes_accessed=1, transcendentals=0),
        name="middle",
    )(col, left_in, left_out, kernel, gain_in[None])
    back = lax.all_to_all(f3, BOTH, 0, 0, tiled=True).reshape(n_seq, n_chan, r_own, own)
    late = [go(aa0, yy), go(ay1, fwd)]
    shape = (inner, full)
    rows_f32, rows_bf = jax.ShapeDtypeStruct(shape, F32), jax.ShapeDtypeStruct(shape, BF)
    room = pltpu.CompilerParams(vmem_limit_bytes=28 << 20)
    cost = pl.CostEstimate(flops=10**11, bytes_accessed=1, transcendentals=0)
    stream, normed = pl.pallas_call(
        third_kernel,
        out_shape=(rows_bf, rows_bf),
        in_specs=[smem, vmem, vmem, any_, vmem, vmem],
        out_specs=(vmem, vmem),
        scratch_shapes=[pltpu.VMEM(shape, F32), pltpu.VMEM(right_out.shape, BF), pltpu.SemaphoreType.DMA],
        compiler_params=room,
        name="third",
    )(place, back, tok, right_out, twiddle_out, gain_mlp[None])

    def mlp(name, rows, before, begun, packs, out):
        packs, spans = zip(*packs)
        count = sum(stop - start for start, stop in spans) // tall
        pieces = sum(-(-(stop - start) // tall) for start, stop in spans)
        return pl.pallas_call(
            functools.partial(mlp_kernel, spans, begun),
            out_shape=out,
            in_specs=[vmem, vmem if begun else any_] + [any_] * len(packs),
            out_specs=vmem,
            scratch_shapes=([] if out is rows_f32 else [pltpu.VMEM(shape, F32)])
            + [
                pltpu.VMEM((count, tall, 2 * hid), BF),
                pltpu.SemaphoreType.DMA((pieces,)),
                pltpu.VMEM((inner, 2 * hid), F32),
                pltpu.VMEM((inner, 2 * hid), F32),
            ],
            compiler_params=room,
            cost_estimate=cost,
            name=name,
        )(rows, before, *packs)

    theirs = go(normed, swap)
    whole = lambda *arrays: [(w, (0, w.shape[1])) for w in arrays]
    early = whole(q0, q1, a_most, a1, y0, y1, ya_most, ay1)
    late = whole(aa0, aa1, *late)
    own_sum = mlp("own", normed, stream, True, early, rows_f32)
    their_sum = mlp("their", theirs, own_sum, False, early, rows_f32)
    partial = go(mlp("their_late", theirs, their_sum, True, late, rows_bf), swap)
    own_sum = mlp("own_late", normed, own_sum, True, late, rows_f32)
    done = pl.pallas_call(
        sum_kernel,
        out_shape=jax.ShapeDtypeStruct((n_chan, inner, own), BF),
        in_specs=[vmem] * 2,
        out_specs=vmem,
        compiler_params=room,
        name="sum",
    )(own_sum, partial)
    out = lax.all_to_all(done, "chan", 0, 0, tiled=True)
    return out.reshape(tokens.shape)


def solution(mesh):
    in_specs = (
        P("seq", "chan"),
        P("chan"),
        P(),
        P("seq", None),
        P(),
        P(None, "seq", "chan"),
        P(),
        P(),
        P("seq", None),
        P(),
        P(None, "chan"),
        P(None, "chan"),
        P("chan", None),
    )
    return jax.shard_map(local, mesh=mesh, in_specs=in_specs, out_specs=P("seq", "chan"), check_vma=False)
```
